32 devices in a mesh: rep: 2 (over y), seq: 4 (over x, core), fsdp: 4 (over z).
Axes of the slice: x: 2, y: 2, z: 4, core: 2. Of those that a mesh axis runs over, the one named last changes fastest.
Arguments:
- tokens: bfloat16 [16, 1024, 2048], P(('rep', 'fsdp'), 'seq'), may hold values from -6 to 6
- doc_start: int32 [16, 1024], P(('rep', 'fsdp'), 'seq'), may hold values from 0 to 1023, as said below
- cotangent: bfloat16 [16, 1024, 2048], P(('rep', 'fsdp'), 'seq'), may hold values from -6 to 6
- norm_gain: bfloat16 [2048], P(('seq', 'fsdp')), may hold values from 0.5 to 1.5
- input_matrix: bfloat16 [2048, 8512], P(('seq', 'fsdp')), may hold values from -0.125 to 0.125
- conv_weight: bfloat16 [4352, 4], P(('seq', 'fsdp')), may hold values from -3 to 3
- conv_bias: bfloat16 [4352], P(('seq', 'fsdp')), may hold values from -3 to 3
- step_bias: bfloat16 [64], P(('seq', 'fsdp')), may hold values from -6 to -4
- decay_log: bfloat16 [64], P(('seq', 'fsdp')), may hold values from -3.5 to 1.09375
- skip_gain: bfloat16 [64], P(('seq', 'fsdp')), may hold values from 0.5 to 1.5
- gate_gain: bfloat16 [4096], P(('seq', 'fsdp')), may hold values from 0.5 to 1.5
- output_matrix: bfloat16 [4096, 2048], P(('seq', 'fsdp')), may hold values from -0.09375 to 0.09375
Outputs:
- layer_out: bfloat16 [16, 1024, 2048], P(('rep', 'fsdp'), 'seq')
- tokens_grad: float32 [16, 1024, 2048], P(('rep', 'fsdp'), 'seq')
- norm_gain_grad: float32 [2048], P(('seq', 'fsdp'))
- in_projection_grad: float32 [2048, 8512], P(('seq', 'fsdp'))
- conv_weight_grad: float32 [4352, 4], P(('seq', 'fsdp'))
- conv_bias_grad: float32 [4352], P(('seq', 'fsdp'))
- step_bias_grad: float32 [64], P(('seq', 'fsdp'))
- decay_log_grad: float32 [64], P(('seq', 'fsdp'))
- skip_gain_grad: float32 [64], P(('seq', 'fsdp'))
- gate_gain_grad: float32 [4096], P(('seq', 'fsdp'))
- out_projection_grad: float32 [4096, 2048], P(('seq', 'fsdp'))
The draws below stay inside these ranges and needn't reach their ends.
Inputs may be any that keep to these rules, and one draw needn't show every extreme that they name: `doc_start`: never falls along a sequence; each value is the position, within its sequence, of the first token of that token's document. In each aligned block of 2 sequences one sequence, drawn from the seed, is a single document; every other sequence ends with a document of one token.
All inputs are finite; a program needn't handle non-finite values.
Results may differ from the reference program's by a relative error of at most 0.013.
Values may be sent and summed in bfloat16 or wider, within the bound.
A program may use at most 248 MiB of HBM per device.

```python
import math
import jax
import jax.numpy as jnp
from jax import lax

D = 2048
DI = 4096
H = 64
PD = 64
N = 128
KW = 4
SPAN = 256
E = 8512
CC = 4352
LOCAL = 2
SEQS = 16
LENGTH = 1024


def draw_doc_start(key, part):
    key = jax.random.fold_in(key, 11)
    rate_key, flag_key, pick_key = jax.random.split(key, 3)
    spacing = jnp.array([8, 32, 128, 512], jnp.int32)
    choose = jax.random.randint(rate_key, (SEQS,), 0, 4)
    per_row = jnp.sum((choose[:, None] == jnp.arange(4, dtype=jnp.int32)[None, :]).astype(jnp.int32) * spacing[None, :], axis=1)
    raw_draws = jax.random.randint(flag_key, (SEQS, LENGTH), 0, 1 << 20)
    begins = raw_draws % per_row[:, None] == 0
    position = jnp.arange(LENGTH, dtype=jnp.int32)
    single = jax.random.randint(pick_key, (SEQS // LOCAL,), 0, LOCAL)
    row_ids = jnp.arange(SEQS, dtype=jnp.int32)
    one_doc = row_ids % LOCAL == single[row_ids // LOCAL]
    begins = (begins | (position[None, :] == LENGTH - 1)) & jnp.logical_not(one_doc)[:, None]
    begins = begins | (position[None, :] == 0)
    starts_at = jnp.where(begins, position[None, :], 0)
    return lax.cummax(starts_at, axis=1).astype(jnp.int32)


def shard_levels(key, dims, cuts, least, high):
    def one(axis_at, blocks):
        heights = jax.random.uniform(jax.random.fold_in(jax.random.fold_in(key, 6), axis_at), (blocks,), jnp.float32, least / len(cuts), high / len(cuts))
        return jnp.repeat(jnp.exp(heights), dims[axis_at] // blocks).reshape((-1,) + (1,) * (len(dims) - axis_at - 1))

    gain = one(*cuts[0])
    for cut in cuts[1:]:
        gain = gain * one(*cut)
    return gain


def centred(key, shape, deviation, reach, shards=(), kind=jnp.bfloat16):
    values = jax.random.normal(key, shape, jnp.float32) * deviation
    if len(shards) > 0:
        values = shard_levels(key, shape, shards, -0.22, 0.18) * values
    return jnp.clip(values, min=-reach, max=reach).astype(kind)


def setup_inputs(seed: int = 0) -> dict:
    key_of = jax.random.split(jax.random.key(seed), 13)
    tokens = centred(key_of[0], (SEQS, LENGTH, D), 1.0, 6.0, ((0, 8), (1, 4)))
    doc_start = draw_doc_start(jax.random.fold_in(key_of[12], 71), 0)
    cotangent = centred(key_of[2], (SEQS, LENGTH, D), 1.0, 6.0, ((0, 8), (1, 4)))
    norm_gain = jnp.clip(1.0 + 0.1 * jax.random.normal(key_of[3], (D,), jnp.float32), 0.5, 1.5).astype(jnp.bfloat16)
    input_matrix = centred(key_of[4], (D, E), D ** -0.5, 0.125, ((0, 16),))
    conv_weight = centred(key_of[5], (CC, KW), KW ** -0.5, 3.0, ((0, 16),))
    conv_bias = centred(key_of[6], (CC,), 0.5, 3.0, ((0, 16),))
    step_bias = jnp.clip(-6.0 + 2.0 * jax.random.uniform(key_of[7], (H,), jnp.float32) ** shard_levels(key_of[7], (H,), ((0, 16),), -0.2, 0.2), -6.0, -4.0).astype(jnp.bfloat16)
    decay_log = jnp.clip(-3.5 + 4.59375 * jax.random.uniform(key_of[8], (H,), jnp.float32) ** shard_levels(key_of[8], (H,), ((0, 16),), -0.2, 0.2), -3.5, 1.09375).astype(jnp.bfloat16)
    skip_gain = jnp.clip(0.5 + 1.0 * jax.random.uniform(key_of[9], (H,), jnp.float32) ** shard_levels(key_of[9], (H,), ((0, 16),), -0.2, 0.2), 0.5, 1.5).astype(jnp.bfloat16)
    gate_gain = jnp.clip(1.0 + 0.1 * jax.random.normal(key_of[10], (DI,), jnp.float32), 0.5, 1.5).astype(jnp.bfloat16)
    output_matrix = centred(key_of[11], (DI, D), DI ** -0.5, 0.09375, ((0, 16),))
    return {"tokens": tokens, "doc_start": doc_start, "cotangent": cotangent, "norm_gain": norm_gain, "input_matrix": input_matrix, "conv_weight": conv_weight, "conv_bias": conv_bias, "step_bias": step_bias, "decay_log": decay_log, "skip_gain": skip_gain, "gate_gain": gate_gain, "output_matrix": output_matrix}


EPSILON = 1e-05
EXACT_MATMUL = lax.Precision.HIGHEST

@jax.custom_vjp
def lowered_value(v):
    return lax.optimization_barrier(v.astype(jnp.bfloat16)).astype(jnp.float32)

@jax.custom_vjp
def lowered_gradient(v):
    return v

def low_keep(v):
    return (lowered_value(v), None)

def low_pass(kept, grad):
    return (grad,)

def back_keep(v):
    return (v, None)

def back_low(kept, grad):
    return (lowered_value(grad),)
lowered_value.defvjp(low_keep, low_pass)
lowered_gradient.defvjp(back_keep, back_low)

def rms_scale(values, gain_vec):
    return values * lax.rsqrt(lax.optimization_barrier(jnp.mean(values * values, axis=-1, keepdims=True)) + EPSILON) * gain_vec

def conv_mix(extended, doc_start, position, conv_weight, conv_bias):
    seq_len = doc_start.shape[1]
    taps = conv_weight.shape[1]
    result = conv_bias
    for offset in range(taps):
        source = position - taps + 1 + offset
        usable = (source[None, :] >= doc_start).astype(jnp.float32)
        result = result + conv_weight[:, offset] * extended[:, offset:offset + seq_len] * usable[..., None]
    return result

def span_mix(carry_state, head_input, write_vec, read_vec, step_size, log_decay, doc_start, begin_at):
    seq_len = head_input.shape[1]
    cum_decay = jnp.cumsum(log_decay, axis=1)
    position = begin_at + jnp.arange(seq_len, dtype=jnp.int32)
    same_doc = ((doc_start[:, :, None] == doc_start[:, None, :]) & (position[:, None] >= position[None, :]))[..., None]
    gaps = cum_decay[:, :, None, :] - cum_decay[:, None, :, :]
    decay_mat = jnp.where(same_doc, jnp.exp(jnp.where(same_doc, gaps, 0.0)), 0.0)
    scores = jnp.einsum('stn,sun->stu', lowered_value(lowered_gradient(read_vec)), lowered_value(lowered_gradient(write_vec)), precision=EXACT_MATMUL)
    mixing = lowered_value(lowered_gradient(scores[..., None] * decay_mat * step_size[:, None, :, :]))
    mixer_out = jnp.einsum('stuh,suhp->sthp', mixing, lowered_value(lowered_gradient(head_input)), precision=EXACT_MATMUL)
    carried = jnp.exp(cum_decay) * (doc_start < begin_at)[..., None]
    mixer_out = mixer_out + jnp.einsum('stn,shpn->sthp', read_vec, carry_state, precision=EXACT_MATMUL) * carried[..., None]
    final_decay = cum_decay[:, -1:, :]
    last_doc = (doc_start == doc_start[:, -1:])[..., None]
    tail_weight = jnp.exp(final_decay - cum_decay) * last_doc * step_size
    through = jnp.exp(final_decay[:, 0]) * (doc_start[:, -1:] < begin_at)
    new_state = jnp.einsum('suh,suhp,sun->shpn', tail_weight, head_input, write_vec, precision=EXACT_MATMUL)
    new_state = new_state + through[:, :, None, None] * carry_state
    return (mixer_out, new_state)

def layer(widened_tokens, doc_start, norm_gain, input_matrix, conv_weight, conv_bias, step_bias, decay_log, skip_gain, gate_gain, output_matrix):
    seqs_here, seq_len, _ = widened_tokens.shape
    channels = conv_weight.shape[0]
    normalized_rows = lowered_value(rms_scale(widened_tokens, norm_gain))
    projected_rows = lowered_value(lowered_gradient(jnp.einsum('oju,uk->ojk', normalized_rows, input_matrix, precision=EXACT_MATMUL)))
    gate_part = projected_rows[..., :DI]
    conv_part = projected_rows[..., DI:DI + channels]
    step_part = projected_rows[..., DI + channels:]
    position = jnp.arange(seq_len, dtype=jnp.int32)
    extended = jnp.pad(conv_part, ((0, 0), (KW - 1, 0), (0, 0)))
    activated = jax.nn.silu(conv_mix(extended, doc_start, position, conv_weight, conv_bias))
    head_input = activated[..., :DI].reshape(seqs_here, seq_len, H, PD)
    write_vec = activated[..., DI:DI + N]
    read_vec = activated[..., DI + N:]
    step_size = jax.nn.softplus(step_part + step_bias)
    log_decay = -jnp.exp(decay_log) * step_size
    blocks = seq_len // SPAN

    def split_blocks(values):
        return jnp.moveaxis(values.reshape((seqs_here, blocks, SPAN) + values.shape[2:]), 1, 0)

    def advance(carry_state, pieces):
        block_out, new_state = span_mix(carry_state, *pieces)
        return (new_state, block_out)
    initial = jnp.zeros((seqs_here, H, PD, N), jnp.float32)
    starts = jnp.arange(blocks, dtype=jnp.int32) * SPAN
    final_state, span_out = lax.scan(jax.checkpoint(advance), initial, (split_blocks(head_input), split_blocks(write_vec), split_blocks(read_vec), split_blocks(step_size), split_blocks(log_decay), split_blocks(doc_start), starts))
    mixer_out = jnp.moveaxis(span_out, 0, 1).reshape(seqs_here, seq_len, H, PD)
    mixer_out = (mixer_out + skip_gain[:, None] * head_input).reshape(seqs_here, seq_len, DI)
    gated = mixer_out * jax.nn.silu(gate_part)
    mixer_result = lowered_value(rms_scale(gated, gate_gain))
    return widened_tokens + jnp.einsum('ucb,by->ucy', mixer_result, output_matrix, precision=EXACT_MATMUL)

def reference(tokens, doc_start, cotangent, norm_gain, input_matrix, conv_weight, conv_bias, step_bias, decay_log, skip_gain, gate_gain, output_matrix):
    weights = tuple((weight_arg.astype(jnp.float32) for weight_arg in (norm_gain, input_matrix, conv_weight, conv_bias, step_bias, decay_log, skip_gain, gate_gain, output_matrix)))
    group = math.gcd(SEQS, max(1, 4096 // LENGTH))
    batches = SEQS // group

    def regroup(values):
        return values.reshape((batches, group) + values.shape[1:])

    def one_group(running, pieces):
        block_tokens, block_docs, block_cotangent = pieces

        def forward(widened_tokens, *params):
            return layer(widened_tokens, block_docs, *params)
        block_out, pullback = jax.vjp(forward, block_tokens.astype(jnp.float32), *weights)
        updates = pullback(block_cotangent.astype(jnp.float32))
        running = tuple((total_part + update for total_part, update in zip(running, updates[1:])))
        return (running, (block_out.astype(jnp.bfloat16), updates[0]))
    initial = tuple((jnp.zeros_like(weight_arg) for weight_arg in weights))
    totals, (layer_outs, token_grads) = lax.scan(one_group, initial, (regroup(tokens), regroup(doc_start), regroup(cotangent)))
    return (layer_outs.reshape(SEQS, LENGTH, D), token_grads.reshape(SEQS, LENGTH, D), totals[0], totals[1], totals[2], totals[3], totals[4], totals[5], totals[6], totals[7], totals[8])
```

```python
import functools

import jax
import jax.numpy as jnp
import numpy as np
from jax import lax
from jax.experimental import pallas as pl
from jax.experimental.pallas import tpu as pltpu
from jax.sharding import Mesh, PartitionSpec as P

DI = 4096
H = 64
PD = 64
N = 128
KW = 4
EPSILON = 1e-05
LANES = 128
BF = jnp.bfloat16
F32 = jnp.float32
FAR = -1e30


def dot(a, b, dims):
    return lax.dot_general(a, b, (dims, ((), ())), preferred_element_type=F32)


def nn(a, b):
    return dot(a, b, ((1,), (0,)))


def nt(a, b):
    return dot(a, b, ((1,), (1,)))


def tn(a, b):
    return dot(a, b, ((0,), (0,)))


def split_rows(v, parts):
    pieces = []
    for _ in range(parts):
        high = v.astype(BF).astype(F32)
        pieces.append(high)
        v = v - high
    return jnp.concatenate(pieces, axis=0).astype(BF)


def running_sum(v, triangle):
    rows = v.shape[0]
    total = nn(split_rows(v, 3), triangle)
    return total[:rows] + total[rows : 2 * rows] + total[2 * rows :]


def softplus(v):
    e = jnp.exp(-jnp.abs(v))
    return jnp.maximum(v, 0.0) + jnp.log1p(e)


def sigmoid(v):
    return 1.0 / (1.0 + jnp.exp(-v))


def column_of_row(row, width):
    high = row.astype(BF).astype(F32)
    rows = lax.broadcasted_iota(jnp.int32, (8, row.shape[1]), 0)
    stack = jnp.where(rows == 0, high, jnp.where(rows == 1, row - high, 0.0)).astype(BF)
    return tn(stack, jnp.ones((8, width), BF))


def scan_front(s, span, x_ref, xt_ref, bc_ref, bct_ref, st_ref, doc_ref, cw_ref, hp_ref, e3_ref, i3_ref, tri_ref, ext):
    ch = x_ref.shape[-1]
    wide = ext.shape[1]
    zero_tail = s == 0
    xt = xt_ref[...].astype(F32)
    bct = bct_ref[...].astype(F32)
    ext[0:16, :ch] = jnp.where(zero_tail, 0.0, xt)
    ext[0:16, ch:] = jnp.where(zero_tail, 0.0, bct)
    ext[16:, :ch] = x_ref[...].astype(F32)
    ext[16:, ch:] = bc_ref[...].astype(F32)
    doc_row = doc_ref[...]
    doc_col = column_of_row(doc_row, LANES)
    begin = s * span
    at = (begin + lax.broadcasted_iota(jnp.int32, (span, LANES), 0)).astype(F32)
    since = at - doc_col
    usable = [(since >= float(KW - 1 - k)).astype(F32) for k in range(KW - 1)]

    def pre_of(c):
        cols = slice(c * LANES, (c + 1) * LANES)
        shifted = [ext[16 - KW + 1 + k : 16 - KW + 1 + k + span, cols] for k in range(KW)]
        masked = [shifted[k] * usable[k] for k in range(KW - 1)] + [shifted[KW - 1]]
        pre = cw_ref[KW : KW + 1, cols]
        for k in range(KW):
            pre = pre + cw_ref[k : k + 1, cols] * masked[k]
        return pre, masked

    heads = hp_ref.shape[0]
    raw = jnp.transpose(st_ref[...].astype(F32))[:heads]
    raw = raw + hp_ref[:, 0:1]
    step = softplus(raw)
    rate = -jnp.exp(hp_ref[:, 1:2])
    log_decay = rate * step
    cum = running_sum(log_decay, tri_ref[...])
    cum_col = tn(split_rows(cum, 3), i3_ref[...])
    last = cum[:, span - 1 : span]
    doc8 = jnp.broadcast_to(doc_row, (heads, span))
    begin_f = begin.astype(F32)
    carried = jnp.where(doc8 < begin_f, jnp.exp(cum), 0.0)
    tail = jnp.where(doc8 == doc_row[:, span - 1 : span], jnp.exp(last - cum), 0.0)
    e3 = e3_ref[...]
    step_x = tn(split_rows(step, 3), e3)
    carried_x = tn(split_rows(carried, 3), e3)
    tail_x = tn(split_rows(tail, 3), e3)
    return dict(
        doc_row=doc_row, doc_col=doc_col, usable=usable, pre_of=pre_of, raw=raw, step=step, rate=rate,
        log_decay=log_decay, cum=cum, cum_col=cum_col, step_x=step_x, carried_x=carried_x, tail_x=tail_x, begin_f=begin_f,
    )


def forward_kernel(x_ref, xt_ref, bc_ref, bct_ref, g_ref, st_ref, doc_ref, cw_ref, hp_ref, sk_ref, e3_ref, i3_ref, tri_ref,
                   y_ref, gated_ref, s1_ref, entry_ref, ext, act, state):
    s = pl.program_id(1)
    span, ch = x_ref.shape
    wide = ext.shape[1]

    @pl.when(s == 0)
    def _():
        state[...] = jnp.zeros_like(state)

    f = scan_front(s, span, x_ref, xt_ref, bc_ref, bct_ref, st_ref, doc_ref, cw_ref, hp_ref, e3_ref, i3_ref, tri_ref, ext)
    for c in range(wide // LANES):
        pre, _ = f["pre_of"](c)
        act[:, c * LANES : (c + 1) * LANES] = pre * sigmoid(pre)
    entry_ref[...] = state[...]
    write = act[:, ch : ch + N].astype(BF)
    read = act[:, ch + N :].astype(BF)
    scores = nt(read, write)
    row = lax.broadcasted_iota(jnp.int32, (span, span), 0)
    col = lax.broadcasted_iota(jnp.int32, (span, span), 1)
    doc_wide = jnp.concatenate([f["doc_col"]] * (span // LANES), axis=1)
    inside = (col.astype(F32) + f["begin_f"] >= doc_wide) & (col <= row)
    bias = jnp.where(inside, 0.0, FAR)
    lane = lax.broadcasted_iota(jnp.int32, (span, LANES), 1)
    per = LANES // PD
    squares = jnp.zeros((span, LANES), F32)
    for j in range(ch // LANES):
        cols = slice(j * LANES, (j + 1) * LANES)
        x = act[:, cols]
        xd = (x * f["step_x"][:, cols]).astype(BF)
        y = jnp.zeros((span, LANES), F32)
        for i in range(per):
            h = j * per + i
            gap = f["cum_col"][:, h : h + 1] - f["cum"][h : h + 1, :] + bias
            mixing = (scores * jnp.exp(gap)).astype(BF)
            y = jnp.where((lane >= i * PD) & (lane < (i + 1) * PD), nn(mixing, xd), y)
        before = state[:, cols]
        y = y + f["carried_x"][:, cols] * nn(read, before.astype(BF))
        y = y + sk_ref[:, cols] * x
        through = f["carried_x"][span - 1 : span, cols]
        built = tn(write, (xd.astype(F32) * f["tail_x"][:, cols]).astype(BF))
        state[:, cols] = through * before + built
        g = g_ref[:, cols].astype(F32)
        gated = y * g * sigmoid(g)
        y_ref[:, cols] = y.astype(BF)
        gated_ref[:, cols] = gated.astype(BF)
        squares = squares + gated * gated
    s1_ref[...] = nt(jnp.ones((8, LANES), BF), squares.astype(BF))


def backward_kernel(x_ref, xt_ref, bc_ref, bct_ref, g_ref, st_ref, doc_ref, cw_ref, hp_ref, sk_ref, e3_ref, i3_ref, tri_ref,
                    low_ref, pick_ref, y_ref, t1_ref, stat_ref, entry_ref,
                    pb_ref, cg_ref, hg_ref, sg_ref,
                    ext, act, dfac, shifted_back, adj, score_back, rows8):
    step_id = pl.program_id(1)
    s = pl.num_programs(1) - 1 - step_id
    span, ch = x_ref.shape
    wide = ext.shape[1]
    heads = hp_ref.shape[0]

    @pl.when(step_id == 0)
    def _():
        adj[...] = jnp.zeros_like(adj)
        shifted_back[...] = jnp.zeros_like(shifted_back)

    @pl.when((step_id == 0) & (pl.program_id(0) == 0))
    def _():
        cg_ref[...] = jnp.zeros_like(cg_ref)
        hg_ref[...] = jnp.zeros_like(hg_ref)
        sg_ref[...] = jnp.zeros_like(sg_ref)

    f = scan_front(s, span, x_ref, xt_ref, bc_ref, bct_ref, st_ref, doc_ref, cw_ref, hp_ref, e3_ref, i3_ref, tri_ref, ext)
    for c in range(wide // LANES):
        cols = slice(c * LANES, (c + 1) * LANES)
        pre, _ = f["pre_of"](c)
        sg = sigmoid(pre)
        act[:, cols] = pre * sg
        dfac[:, cols] = sg * (1.0 + pre * (1.0 - sg))
    write = act[:, ch : ch + N].astype(BF)
    read = act[:, ch + N :].astype(BF)
    scores_t = nt(write, read)
    row = lax.broadcasted_iota(jnp.int32, (span, span), 0)
    col = lax.broadcasted_iota(jnp.int32, (span, span), 1)
    inside = (row.astype(F32) + f["begin_f"] >= f["doc_row"]) & (row <= col)
    bias = jnp.where(inside, 0.0, FAR)
    lane = lax.broadcasted_iota(jnp.int32, (span, LANES), 1)
    lane1 = lax.broadcasted_iota(jnp.int32, (1, LANES), 1)
    last1 = lax.broadcasted_iota(jnp.int32, (1, span), 1) == span - 1
    per = LANES // PD
    stat = tn(split_rows(stat_ref[...], 3), pick_ref[...])
    inv = stat[:, :LANES]
    kk = stat[:, LANES:]
    score_back[...] = jnp.zeros_like(score_back)
    head_rows = jnp.zeros((heads, span), F32)
    size_rows = jnp.zeros((heads, span), F32)
    write_back = jnp.zeros((span, N), F32)
    read_back = jnp.zeros((span, N), F32)
    for j in range(ch // LANES):
        cols = slice(j * LANES, (j + 1) * LANES)
        x = act[:, cols]
        step_x = f["step_x"][:, cols]
        tail_x = f["tail_x"][:, cols]
        carried_x = f["carried_x"][:, cols]
        xd = (x * step_x).astype(BF)
        g = g_ref[:, cols].astype(F32)
        y = y_ref[:, cols].astype(F32)
        sg = sigmoid(g)
        silu = g * sg
        gated_back = inv * t1_ref[:, cols].astype(F32) - kk * (y * silu)
        dy = gated_back * silu
        pb_ref[:, ch + j * LANES : ch + (j + 1) * LANES] = (gated_back * y * (sg * (1.0 + g * (1.0 - sg)))).astype(BF)
        dyb = dy.astype(BF)
        sg_ref[0:1, cols] += jnp.sum(dy * x, axis=0, keepdims=True)
        before = entry_ref[:, cols]
        before_b = before.astype(BF)
        after = adj[:, cols]
        after_b = after.astype(BF)
        through = carried_x[span - 1 : span, :]
        dyc = (dy * carried_x).astype(BF)
        carry_y = carried_x * nn(read, before_b)
        read_back = read_back + nt(dyc, before_b)
        tail_back = tail_x * nn(write, after_b)
        xd_f = xd.astype(F32)
        write_back = write_back + nt((xd_f * tail_x).astype(BF), after_b)
        ends = through * jnp.sum(after * before, axis=0, keepdims=True) + jnp.sum(xd_f * tail_back, axis=0, keepdims=True)
        adj[:, cols] = through * after + tn(read, dyc)
        xd_back = tail_back
        for i in range(per):
            h = j * per + i
            mine = (lane >= i * PD) & (lane < (i + 1) * PD)
            gap = f["cum"][h : h + 1, :] - f["cum_col"][:, h : h + 1] + bias
            decay = jnp.exp(gap)
            mixing = (scores_t * decay).astype(BF)
            mixing_back = nt(jnp.where(mine, xd, jnp.zeros_like(xd)), dyb)
            score_back[...] += mixing_back * decay
            sums = jnp.sum(mixing_back * mixing.astype(F32), axis=0, keepdims=True)
            mine1 = (lane1 >= i * PD) & (lane1 < (i + 1) * PD)
            end = jnp.sum(jnp.where(mine1, ends, 0.0), axis=1, keepdims=True)
            rows8[h : h + 1, :] = sums + jnp.where(last1, end, 0.0)
            xd_back = xd_back + jnp.where(mine, nn(mixing, dyb), 0.0)
        act_back = sk_ref[:, cols] * dy + step_x * xd_back
        part = dy * carry_y - xd_f * xd_back
        high = part.astype(BF)
        low = (part - high.astype(F32)).astype(BF)
        e1 = e3_ref[0:heads, cols]
        head_rows = head_rows + nt(e1, high) + nt(e1, low)
        size_rows = size_rows + nt(e1, (x * xd_back).astype(BF))
        dfac[:, cols] = dfac[:, cols] * act_back
    sb = score_back[...].astype(BF)
    write_back = write_back + nn(sb, read)
    read_back = read_back + tn(sb, write)
    dfac[:, ch : ch + N] = dfac[:, ch : ch + N] * write_back
    dfac[:, ch + N :] = dfac[:, ch + N :] * read_back

    decay_back = running_sum(rows8[0:heads, :] + head_rows, low_ref[...])
    at_row = (s * span).astype(F32) + lax.broadcasted_iota(jnp.int32, (heads, span), 1).astype(F32)
    decay_back = jnp.where(at_row > f["doc_row"], decay_back, 0.0)
    step_back = (size_rows + f["rate"] * decay_back) * sigmoid(f["raw"])
    hg_ref[0:heads, :] += step_back
    hg_ref[heads : 2 * heads, :] += decay_back * f["log_decay"]
    padded = jnp.concatenate([step_back, jnp.zeros((LANES - heads, span), F32)], axis=0)
    pb_ref[:, 2 * ch + 2 * N :] = jnp.transpose(padded).astype(BF)

    for c in range(wide // LANES):
        cols = slice(c * LANES, (c + 1) * LANES)
        _, masked = f["pre_of"](c)
        pre_back = dfac[:, cols]
        for k in range(KW):
            cg_ref[k : k + 1, cols] += jnp.sum(pre_back * masked[k], axis=0, keepdims=True)
        cg_ref[KW : KW + 1, cols] += jnp.sum(pre_back, axis=0, keepdims=True)
        back = cw_ref[KW - 1 : KW, cols] * pre_back
        for k in range(KW - 1):
            z = pre_back * f["usable"][k]
            shifted_back[k, 0:span, cols] = z
            back = back + cw_ref[k : k + 1, cols] * shifted_back[k, KW - 1 - k : KW - 1 - k + span, cols]
            shifted_back[k, span : span + 8, cols] = z[0:8]
        out = c * LANES if c * LANES < ch else c * LANES + ch
        pb_ref[:, out : out + LANES] = back.astype(BF)


def scan_specs(rp, seqs, local, span, ch, backward):
    def block(s):
        return seqs - 1 - s if backward else s

    def tokens_of(width, at):
        return pl.BlockSpec((None, None, None, span, width), lambda q, s: (q // local, block(s), q % local, 0, at))

    def tail_of(width, at):
        return pl.BlockSpec(
            (None, None, None, 16, width),
            lambda q, s: (q // local, jnp.maximum(block(s) - 1, 0), q % local, span // 16 - 1, at),
        )

    def whole(*shape):
        return pl.BlockSpec(shape, lambda q, s: (0,) * len(shape))

    def rows_of(rows):
        return pl.BlockSpec((None, None, None, rows, span), lambda q, s: (q // local, block(s), q % local, 0, 0))

    def state_of():
        return pl.BlockSpec((None, None, None, N, ch), lambda q, s: (q // local, block(s), q % local, 0, 0))

    return tokens_of, tail_of, whole, rows_of, state_of


def constants(heads, ch, span):
    e = np.repeat(np.eye(heads, dtype=np.float32), PD, axis=1)
    i = np.eye(heads, LANES, dtype=np.float32)
    upper = np.triu(np.ones((span, span), np.float32))
    pick = np.zeros((8, 2 * LANES), np.float32)
    pick[0, :LANES] = 1.0
    pick[1, LANES:] = 1.0
    return tuple(jnp.asarray(v, BF) for v in (np.tile(e, (3, 1)), np.tile(i, (3, 1)), upper, upper.T, np.tile(pick, (3, 1))))


def front_specs(specs, ch, heads, span):
    tokens_of, tail_of, whole, rows_of, _ = specs
    wide = ch + 2 * N
    return [
        tokens_of(ch, 0), tail_of(ch, 0), tokens_of(2 * N, 2 * ch // (2 * N)), tail_of(2 * N, 2 * ch // (2 * N)),
        tokens_of(ch, 1), tokens_of(LANES, (2 * ch + 2 * N) // LANES), rows_of(1),
        whole(8, wide), whole(heads, LANES), whole(1, ch), whole(3 * heads, ch), whole(3 * heads, LANES), whole(span, span),
    ]


def mixer_forward(proj, doc, cw, hp, sk, consts):
    rp, seqs, local, span, _ = proj.shape
    heads, ch = hp.shape[0], sk.shape[1]
    wide = ch + 2 * N
    specs = scan_specs(rp, seqs, local, span, ch, False)
    tokens_of, tail_of, whole, rows_of, state_of = specs
    lead = (rp, seqs, local)
    e3, i3, upper, _, _ = consts
    return pl.pallas_call(
        forward_kernel,
        grid=(rp * local, seqs),
        in_specs=front_specs(specs, ch, heads, span),
        out_specs=[tokens_of(ch, 0), tokens_of(ch, 0), rows_of(8), state_of()],
        out_shape=[
            jax.ShapeDtypeStruct(lead + (span, ch), BF),
            jax.ShapeDtypeStruct(lead + (span, ch), BF),
            jax.ShapeDtypeStruct(lead + (8, span), F32),
            jax.ShapeDtypeStruct(lead + (N, ch), F32),
        ],
        scratch_shapes=[pltpu.VMEM((span + 16, wide), F32), pltpu.VMEM((span, wide), F32), pltpu.VMEM((N, ch), F32)],
        compiler_params=pltpu.CompilerParams(vmem_limit_bytes=40 * 2**20),
        cost_estimate=pl.CostEstimate(flops=20 * 10**9, bytes_accessed=30 * 10**6, transcendentals=0),
        name="mixer_forward",
    )(proj, proj, proj, proj, proj, proj, doc, cw, hp, sk, e3, i3, upper)


def mixer_backward(proj, doc, cw, hp, sk, consts, y, t1, stat, entry):
    rp, seqs, local, span, columns = proj.shape
    heads, ch = hp.shape[0], sk.shape[1]
    wide = ch + 2 * N
    specs = scan_specs(rp, seqs, local, span, ch, True)
    tokens_of, tail_of, whole, rows_of, state_of = specs
    lead = (rp, seqs, local)
    e3, i3, upper, lower, pick = consts
    return pl.pallas_call(
        backward_kernel,
        grid=(rp * local, seqs),
        in_specs=front_specs(specs, ch, heads, span)
        + [whole(span, span), whole(24, 2 * LANES), tokens_of(ch, 0), tokens_of(ch, 0), rows_of(8), state_of()],
        out_specs=[tokens_of(columns, 0), whole(8, wide), whole(2 * heads, span), whole(8, ch)],
        out_shape=[
            jax.ShapeDtypeStruct(lead + (span, columns), BF),
            jax.ShapeDtypeStruct((8, wide), F32),
            jax.ShapeDtypeStruct((2 * heads, span), F32),
            jax.ShapeDtypeStruct((8, ch), F32),
        ],
        scratch_shapes=[
            pltpu.VMEM((span + 16, wide), F32), pltpu.VMEM((span, wide), F32), pltpu.VMEM((span, wide), F32),
            pltpu.VMEM((KW - 1, span + 8, wide), F32), pltpu.VMEM((N, ch), F32), pltpu.VMEM((span, span), F32),
            pltpu.VMEM((8, span), F32),
        ],
        compiler_params=pltpu.CompilerParams(vmem_limit_bytes=48 * 2**20),
        cost_estimate=pl.CostEstimate(flops=60 * 10**9, bytes_accessed=60 * 10**6, transcendentals=0),
        name="mixer_backward",
    )(proj, proj, proj, proj, proj, proj, doc, cw, hp, sk, e3, i3, upper, lower, pick, y, t1, stat, entry)


def per_device(tokens, doc_start, cotangent, norm_gain, input_matrix, conv_weight, conv_bias, step_bias, decay_log, skip_gain,
               gate_gain, output_matrix):
    rp, seqs, fs, groups = (lax.axis_size(a) for a in ("rep", "seq", "fsdp", "group"))
    r, s, z = (lax.axis_index(a) for a in ("rep", "seq", "fsdp"))
    local, span, width = tokens.shape
    mine = local * span
    tp = rp * seqs
    heads = H // tp
    ch = heads * PD
    cc = DI + 2 * N
    part = s * rp + r
    plane = ("rep", "seq")
    rows = input_matrix.shape[0]
    out_rows = output_matrix.shape[0]
    conv_rows = conv_weight.shape[0]
    head_rows = step_bias.shape[0]

    doc_f = doc_start.astype(F32).reshape(-1)
    small = [conv_weight.astype(F32).reshape(-1), conv_bias.astype(F32), step_bias.astype(F32), decay_log.astype(F32),
             skip_gain.astype(F32), doc_f]
    small = jnp.concatenate(small)
    small = jnp.pad(small, (0, -small.shape[0] % 1024)).reshape(1, 1, 1, -1)
    everything = lax.all_gather(small, ("rep", "seq", "fsdp"), axis=0, tiled=True).reshape(rp, seqs, fs, -1)
    at = 0

    def taken(count):
        nonlocal at
        at += count
        return everything[0, :, :, at - count : at].reshape(-1)

    conv_w = taken(conv_rows * KW).reshape(cc, KW)
    conv_b = taken(conv_rows)
    bias_all, log_all, skip_all = taken(head_rows), taken(head_rows), taken(head_rows)
    doc = lax.dynamic_index_in_dim(everything[..., at : at + mine], z, axis=2, keepdims=False)
    doc = doc.reshape(rp, seqs, local, 1, span)
    table = jnp.concatenate([conv_w.T, conv_b[None], jnp.zeros((8 - KW - 1, cc), F32)], axis=0)
    cw = jnp.concatenate([lax.dynamic_slice_in_dim(table, part * ch, ch, axis=1), table[:, DI:]], axis=1)
    hp = jnp.stack([bias_all, log_all], axis=1)
    hp = jnp.pad(lax.dynamic_slice_in_dim(hp, part * heads, heads, axis=0), ((0, 0), (0, LANES - 2)))
    sk = jnp.repeat(lax.dynamic_slice_in_dim(skip_all, part * heads, heads, axis=0), PD)[None]
    consts = constants(heads, ch, span)

    wide_tokens = tokens.astype(F32).reshape(mine, width)
    inv_in = lax.rsqrt(jnp.mean(wide_tokens * wide_tokens, axis=-1, keepdims=True) + EPSILON)
    unit = wide_tokens * inv_in
    u = unit.astype(BF).reshape(mine, seqs, fs, rows).swapaxes(1, 2).reshape(mine, width)
    all_u = lax.all_gather(u, plane, axis=0, tiled=True)

    gain = norm_gain.astype(F32)[:, None]
    scaled = (input_matrix.astype(F32) * gain).astype(BF)

    def columns_of(values, each):
        split = values.reshape(rows, seqs, rp, each)
        return lax.dynamic_index_in_dim(split, r, axis=2, keepdims=False)

    pieces = [
        columns_of(scaled[:, DI : 2 * DI], ch), columns_of(scaled[:, :DI], ch),
        jnp.broadcast_to(scaled[:, None, 2 * DI : 2 * DI + 2 * N], (rows, seqs, 2 * N)),
        columns_of(scaled[:, 2 * DI + 2 * N :], heads), jnp.zeros((rows, seqs, LANES - heads), BF),
    ]
    sent = jnp.concatenate(pieces, axis=-1).swapaxes(0, 1)
    columns = sent.shape[-1]
    w_in = lax.all_to_all(sent, "seq", 0, 0, tiled=True)
    w_in = lax.all_gather(w_in, "fsdp", axis=0, tiled=True).reshape(width, columns)

    gate = gate_gain.astype(F32)[:, None]
    scaled_out = (output_matrix.astype(F32) * gate).astype(BF)
    w_out = lax.all_gather(scaled_out, "fsdp", axis=0, tiled=True)
    w_out = lax.dynamic_slice_in_dim(w_out, r * ch, ch, axis=0)
    all_cot = lax.all_gather(cotangent.reshape(mine, width), plane, axis=0, tiled=True)

    proj = nn(all_u, w_in).astype(BF).reshape(rp, seqs, local, span, columns)
    y, gated, s1, entry = mixer_forward(proj, doc, cw, hp, sk, consts)
    count = tp * mine
    gated = gated.reshape(count, ch)
    t1 = nt(all_cot, w_out)
    s2 = jnp.sum(t1 * gated.astype(F32), axis=-1).reshape(rp, seqs, local, span)
    stats = lax.psum(jnp.stack([s1[..., 0, :], s2]), plane)
    inv = lax.rsqrt(stats[0] * (1.0 / DI) + EPSILON)
    kk = inv * inv * inv * stats[1] * (1.0 / DI)
    stat = jnp.pad(jnp.stack([inv, kk], axis=3), ((0, 0),) * 3 + ((0, 6), (0, 0)))

    branch = lax.psum_scatter(nn(gated, w_out).astype(BF), plane, scatter_dimension=0, tiled=True)
    own_inv = lax.dynamic_slice(inv, (r, s, 0, 0), (1, 1, local, span)).reshape(mine, 1)
    layer_out = (wide_tokens + branch.astype(F32) * own_inv).astype(BF).reshape(tokens.shape)

    mixed = (gated.astype(F32) * inv.reshape(count, 1)).astype(BF)
    out_part = tn(mixed, all_cot).astype(BF)

    pb, cg, hg, sg = mixer_backward(proj, doc, cw, hp, sk, consts, y, t1.astype(BF).reshape(y.shape), stat, entry)
    pb = pb.reshape(count, columns)
    back = lax.psum_scatter(nt(pb, w_in).astype(BF), plane, scatter_dimension=0, tiled=True)
    in_part = tn(all_u, pb).astype(BF)

    piece = ch // fs
    out_sum = lax.psum_scatter(out_part, "fsdp", scatter_dimension=0, tiled=True)
    out_sum = lax.all_gather(out_sum, plane[0], axis=0, tiled=False) if False else out_sum
    out_all = lax.all_gather(out_sum, ("rep", "fsdp"), axis=0, tiled=True)
    out_own = lax.dynamic_slice_in_dim(out_all, z * out_rows, out_rows, axis=0).astype(F32)

    in_sum = lax.psum_scatter(in_part, "fsdp", scatter_dimension=0, tiled=True)
    in_sum = lax.all_to_all(in_sum.reshape(seqs, rows, columns), "seq", 0, 0, tiled=True)
    shared = jnp.sum(in_sum[:, :, 2 * ch : 2 * ch + 2 * N].astype(F32), axis=0)
    in_both = lax.all_gather(in_sum, "rep", axis=0)
    shared = lax.psum(shared, "rep")
    in_both = in_both.transpose(2, 1, 0, 3)

    def back_columns(begin, each):
        return in_both[..., begin : begin + each].reshape(rows, tp * each).astype(F32)

    in_own = jnp.concatenate([back_columns(ch, ch), back_columns(0, ch), shared, back_columns(2 * ch + 2 * N, heads)], axis=1)

    conv_grad = jnp.zeros((KW + 1, cc), F32)
    conv_grad = lax.dynamic_update_slice_in_dim(conv_grad, cg[: KW + 1, :ch], part * ch, axis=1)
    conv_grad = lax.dynamic_update_slice_in_dim(conv_grad, cg[: KW + 1, ch:], DI, axis=1)
    by_head = jnp.stack([jnp.sum(hg[:heads], axis=1), jnp.sum(hg[heads:], axis=1), jnp.sum(sg[0].reshape(heads, PD), axis=1)])
    head_grad = lax.dynamic_update_slice_in_dim(jnp.zeros((3, H), F32), by_head, part * heads, axis=1)
    packed = jnp.concatenate([conv_grad.reshape(-1), head_grad.reshape(-1)])
    size = packed.shape[0]
    packed = jnp.pad(packed, (0, -size % 1024)).reshape(-1, LANES)
    packed = lax.psum(packed, ("group", "rep", "seq", "fsdp")).reshape(-1)
    conv_grad = packed[: (KW + 1) * cc].reshape(KW + 1, cc)
    head_grad = packed[(KW + 1) * cc : size].reshape(3, H)
    owner = s * fs + z
    conv_own = lax.dynamic_slice_in_dim(conv_grad, owner * conv_rows, conv_rows, axis=1)
    head_own = lax.dynamic_slice_in_dim(head_grad, owner * head_rows, head_rows, axis=1)

    if groups > 1:
        out_own, in_own = lax.psum((out_own, in_own), "group")
    weight = input_matrix.astype(F32)
    norm_gain_grad = jnp.sum(weight * in_own, axis=1)
    in_own = in_own * gain
    gate_gain_grad = jnp.sum(output_matrix.astype(F32) * out_own, axis=1)
    out_own = out_own * gate

    v = back.astype(F32).reshape(mine, fs, seqs, rows).swapaxes(1, 2).reshape(mine, width)
    tokens_grad = cotangent.astype(F32).reshape(mine, width) + inv_in * (v - unit * jnp.mean(v * unit, axis=-1, keepdims=True))

    return (
        layer_out, tokens_grad.reshape(tokens.shape), norm_gain_grad, in_own, conv_own[:KW].T, conv_own[KW], head_own[0], head_own[1],
        head_own[2], gate_gain_grad, out_own,
    )


def solution(mesh):
    rep, seqs, fs = (mesh.shape[a] for a in ("rep", "seq", "fsdp"))
    pair = 2 if rep % 2 == 0 else 1
    devices = np.asarray(mesh.devices).reshape(rep // pair, pair, seqs, fs)
    planes = Mesh(devices, ("group", "rep", "seq", "fsdp"))
    batch = ("group", "rep", "fsdp")
    by_token = P(batch, "seq", None)
    vector = P(("seq", "fsdp"))
    matrix = P(("seq", "fsdp"), None)
    return jax.shard_map(
        per_device,
        mesh=planes,
        in_specs=(by_token, P(batch, "seq"), by_token, vector, matrix, matrix, vector, vector, vector, vector, vector, matrix),
        out_specs=(by_token, by_token, vector, matrix, matrix, vector, vector, vector, vector, vector, matrix),
        check_vma=False,
    )
```
